32 devices in a mesh: pair: 8 (over z, x), sect: 4 (over y, core).
Axes of the slice: x: 2, y: 2, z: 4, core: 2. Of those that a mesh axis runs over, the one named last changes fastest.
Arguments:
- operators: float32 [16, 1024, 1024], P('pair', 'sect'), may hold values from -6 to 6
- rotations: float32 [8, 1024, 768], P('pair', 'sect'), may hold values from -0.1875 to 0.1875
- sector_owner: int32 [1], replicated, may hold values from 0 to 7
- slot_pair: int32 [16], replicated, may hold values from 0 to 15, each once
- sources: int32 [16, 16], replicated, may hold values from 0 to 15
- integrals: float32 [16, 16], replicated, may hold values from -3 to 3
- term_count: int32 [16], replicated, may hold values from 1 to 16, 64 in all
Outputs:
- complement: float32 [16, 768, 768], P('pair', 'sect')
The draws below stay inside these ranges and needn't reach their ends.
Inputs may be any that keep to these rules, and one draw needn't show every extreme that they name: `sector_owner`: a pair index along the pair axis. `slot_pair`: each orbital-pair id appears once. `sources`: ids may repeat within a list. `term_count`: the counts sum to 64 and the largest is exactly 16.
All inputs are finite; a program needn't handle non-finite values.
Results may differ from the reference program's by a relative error of at most 0.0001.
Values sent between devices are 32-bit elements; how exact they have to be, the bound alone decides.
A program may use at most 64 MiB of HBM per device.

```python
import math
import jax
import jax.numpy as jnp
import numpy as np
from jax import lax

M = 1024
MNEW = 768
R = 16
N_OPS = 16
N_PAIR = 8


def touch_ends(result, stream_key, least, high):
    longest = result.shape.index(max(result.shape))
    spots = []
    for shift in (0, 1):
        where = [jax.random.randint(jax.random.fold_in(stream_key, axis), (), 0, length) for axis, length in enumerate(result.shape)]
        where[longest] = (where[longest] + shift) % result.shape[longest]
        spots.append(tuple(where))
    return result.at[spots[0]].set(least).at[spots[1]].set(high)


def steps_of(stream_key, extent, shards, low, largest):
    loudness, own = 1.0, jax.random.fold_in(stream_key, 6)
    for position, shards_of in shards:
        heights = jnp.exp(jax.random.uniform(jax.random.fold_in(own, position), (shards_of,), jnp.float32, low / len(shards), largest / len(shards)))
        loudness = loudness * jnp.repeat(heights, extent[position] // shards_of).reshape([-1 if axis == position else 1 for axis in range(len(extent))])
    return loudness


def profile(amount, total, bound, skew):
    portions = [(1 << 20) // math.isqrt(standing ** skew) + 1 for standing in range(2, amount + 1)]
    rest, holding = total - bound - (amount - 1), [1] * (amount - 1)
    while rest > 0:
        candidates = [i for i in range(amount - 1) if holding[i] < bound]
        whole, remaining = sum([portions[i] for i in candidates]), rest
        for i in candidates:
            extra = min(bound - holding[i], max(1, remaining * portions[i] // whole), rest)
            holding[i] = holding[i] + extra
            rest = rest - extra
    return np.array([bound] + holding)


def uneven_parts(key, count, total, limit, slope):
    if count == 2:
        one = jax.random.randint(key, (), max(1, total - limit), min(limit, total - 1) + 1)
        return jnp.stack([one, total - one])
    tallies = jnp.asarray(profile(count, total, limit, slope), jnp.int32)
    pairs = (count - 1) // 2
    donor, sink = tallies[1:1 + 2 * pairs:2], tallies[2:2 + 2 * pairs:2]
    room = jnp.minimum(donor - 1, limit - sink)
    passed = jax.random.randint(jax.random.fold_in(key, 1), (pairs,), 0, 1 << 20) % (room + 1)
    tallies = tallies.at[1:1 + 2 * pairs:2].set(donor - passed).at[2:2 + 2 * pairs:2].set(sink + passed)
    return tallies[jax.random.permutation(jax.random.fold_in(key, 2), count)]


def gaussian(own_key, extent, spread, limit, split=(), kind=jnp.bfloat16):
    entries = jax.random.normal(own_key, extent, jnp.float32) * spread
    if len(split) > 0:
        entries = steps_of(own_key, extent, split, -0.22, 0.18) * entries
    return jnp.clip(entries, min=-limit, max=limit).astype(kind)


def setup_inputs(seed: int = 0) -> dict:
    arg_keys = jax.random.split(jax.random.key(seed), 8)
    return {
        "operators": gaussian(arg_keys[0], (N_OPS, M, M), 1.0, 6.0, ((0, 8), (1, 4)), jnp.float32),
        "rotations": gaussian(arg_keys[1], (N_PAIR, M, MNEW), M ** -0.5, 0.1875, ((0, 8), (1, 4)), jnp.float32),
        "sector_owner": jax.random.randint(arg_keys[2], (1,), 0, N_PAIR).astype(jnp.int32),
        "slot_pair": jax.random.permutation(arg_keys[3], N_OPS).astype(jnp.int32),
        "sources": touch_ends(jax.random.randint(arg_keys[4], (N_OPS, R), 0, N_OPS), jax.random.fold_in(arg_keys[4], 1), 0, N_OPS - 1).astype(jnp.int32),
        "integrals": gaussian(arg_keys[5], (N_OPS, R), 0.5, 3.0, (), jnp.float32),
        "term_count": uneven_parts(arg_keys[6], N_OPS, 4 * N_OPS, R, 2).astype(jnp.int32),
    }


def coupling_matrix(slot_pair, sources, integrals, term_count):
    is_live = lax.broadcasted_iota(jnp.int32, sources.shape, 1) < term_count[:, None]
    weighted = jnp.where(is_live, integrals, jnp.zeros_like(integrals))
    matches = (sources[:, :, None] == slot_pair[None, None, :]).astype(integrals.dtype)
    return jnp.sum(weighted[:, :, None] * matches, axis=1)


def reference(operators, rotations, sector_owner, slot_pair, sources, integrals, term_count):
    rotation = lax.dynamic_index_in_dim(rotations, sector_owner[0], 0, keepdims=False)

    def renormalize(operator):
        half_done = jnp.dot(operator, rotation, precision=lax.Precision.HIGHEST, preferred_element_type=jnp.float32)
        return jnp.dot(rotation.T, half_done, precision=lax.Precision.HIGHEST, preferred_element_type=jnp.float32)

    renormalized = lax.map(renormalize, operators)
    coupling = coupling_matrix(slot_pair, sources, integrals, term_count)
    flattened = renormalized.reshape(renormalized.shape[0], -1)
    mixture = jnp.dot(coupling, flattened, precision=lax.Precision.HIGHEST, preferred_element_type=jnp.float32)
    return mixture.reshape(renormalized.shape)
```

```python
import functools

import jax
import jax.numpy as jnp
from jax import lax
from jax.experimental import pallas as pl
from jax.experimental.pallas import tpu as pltpu
from jax.sharding import PartitionSpec as P

F32, BF16 = jnp.float32, jnp.bfloat16
CHUNKS = 4


def broadcast(value, axis, root):
    mine = lax.axis_index(axis) == root
    return lax.psum(jnp.where(mine, value, jnp.zeros_like(value)), axis)


def coupling_matrix(slot_pair, sources, integrals, term_count):
    is_live = lax.broadcasted_iota(jnp.int32, sources.shape, 1) < term_count[:, None]
    weighted = jnp.where(is_live, integrals, jnp.zeros_like(integrals))
    matches = (sources[:, :, None] == slot_pair[None, None, :]).astype(jnp.float32)
    return jnp.sum(weighted[:, :, None] * matches, axis=1)


def split(value):
    high = value.astype(BF16)
    return high, (value - high.astype(F32)).astype(BF16)


def dot3(ah, al, bh, bl):
    dot = functools.partial(jnp.dot, preferred_element_type=F32)
    return dot(ah, bh) + (dot(ah, bl) + dot(al, bh))


def kernel(
    n_pair, owner_ref, coup_ref, ops_ref, rot_ref, out_ref,
    oh, ol, xbuf, cand, zr, zl, sr, sl, rfull, rh, rl, rth, rtl, rdh, rdl,
    sib_out, sib_in, own, y_out, y_in, a_out, a_in, b_out,
    x_s, x_r, zr_s, zr_r, zl_s, zl_r, px_s, px_r, py_s, py_r, pc_s, pc_r,
    c_s, c_r, y_s, y_r, a_s, a_r, b_s, b_r,
):
    local, block, width = ops_ref.shape
    wide = rot_ref.shape[1]
    half = block // 2
    chunk = half // CHUNKS
    new_rows = wide // 4
    piece = new_rows // n_pair
    depth = n_pair // 2
    p, s = lax.axis_index("pair"), lax.axis_index("sect")
    z, x = lax.div(p, 2), lax.rem(p, 2)
    y, c = lax.div(s, 2), lax.rem(s, 2)

    def dev(pp, ss):
        return {"pair": pp, "sect": ss}

    x_nb = dev(p + 1 - 2 * x, s)
    y_nb = dev(p, s + 2 - 4 * y)
    c_nb = dev(p, s + 1 - 2 * c)
    z_up, z_dn = dev(p + 2, s), dev(p - 2, s)

    def copy(src, dst, ssem, rsem, device):
        return pltpu.make_async_remote_copy(
            src_ref=src, dst_ref=dst, send_sem=ssem, recv_sem=rsem,
            device_id=device, device_id_type=pl.DeviceIdType.MESH,
        )

    def rows(start, size, step=8):
        if not isinstance(start, int):
            start = pl.multiple_of(start, step)
        return pl.ds(start, size)

    barrier = pltpu.get_barrier_semaphore()
    for m in range(1, n_pair):
        pl.semaphore_signal(barrier, inc=1, device_id=dev(lax.rem(p + m, n_pair), s),
                            device_id_type=pl.DeviceIdType.MESH)
    for nb in (y_nb, c_nb):
        pl.semaphore_signal(barrier, inc=1, device_id=nb, device_id_type=pl.DeviceIdType.MESH)

    @pl.when(z == 0)
    def _():
        zr[...] = jnp.zeros_like(zr)

    @pl.when(z == depth - 1)
    def _():
        zl[...] = jnp.zeros_like(zl)

    pl.semaphore_wait(barrier, n_pair + 1)

    def x_copy(k):
        return copy(rot_ref.at[rows((1 - x) * half + k * chunk, chunk)],
                    xbuf.at[rows(k * chunk, chunk)], x_s.at[k], x_r.at[k], x_nb)

    for k in range(CHUNKS):
        x_copy(k).start()

    for g in range(local):
        for r in range(2):
            at = pl.ds(r * half, half)
            to = pl.ds(g * block + r * half, half)
            oh[to], ol[to] = split(ops_ref[g, at])

    owner = owner_ref[0]
    owner_z, owner_x = lax.div(owner, 2), lax.rem(owner, 2)

    def r_copy(k):
        at = rows(k * chunk, chunk)
        return copy(sr.at[at], zr.at[at], zr_s.at[k], zr_r.at[k], z_up)

    def l_copy(k):
        at = rows(k * chunk, chunk)
        return copy(sl.at[at], zl.at[at], zl_s.at[k], zl_r.at[k], z_dn)

    def place(yy, cc, xx, k):
        return rows((yy * 2 + cc) * block + xx * half + k * chunk, chunk)

    def p_copy(at, sends, recvs, i, device):
        return copy(rfull.at[at], rfull.at[at], sends.at[i], recvs.at[i], device)

    def refine(yy, cc, xx):
        at = rows((yy * 2 + cc) * block + xx * half, half, 16)
        rh[at], rl[at] = split(rfull[at])

    far = jnp.maximum(z, depth - 1 - z)
    for t in range(CHUNKS + depth - 1):
        if t < CHUNKS:
            x_copy(t).wait_recv()
            at = rows(t * chunk, chunk)
            mine = rot_ref[rows(x * half + t * chunk, chunk)]
            cand[at] = jnp.where(owner_x == x, mine, xbuf[at])
        kr, kl, kf = t - z, t - (depth - 1 - z), t - far

        @pl.when((kr >= 0) & (kr < CHUNKS))
        def _():
            at = rows(kr * chunk, chunk)

            @pl.when(z > 0)
            def _():
                r_copy(kr).wait_recv()

            @pl.when(z < depth - 1)
            def _():
                sr[at] = jnp.where(owner_z == z, cand[at], zr[at])
                r_copy(kr).start()

        @pl.when((kl >= 0) & (kl < CHUNKS))
        def _():
            at = rows(kl * chunk, chunk)

            @pl.when(z < depth - 1)
            def _():
                l_copy(kl).wait_recv()

            @pl.when(z > 0)
            def _():
                sl[at] = jnp.where(owner_z == z, cand[at], zl[at])
                l_copy(kl).start()

        @pl.when((kf >= 0) & (kf < CHUNKS))
        def _():
            at = rows(kf * chunk, chunk)
            to = place(y, c, x, kf)
            rfull[to] = jnp.where(owner_z == z, cand[at], jnp.where(owner_z < z, zr[at], zl[at]))
            p_copy(to, px_s, px_r, kf, x_nb).start()
            p_copy(to, py_s, py_r, kf, y_nb).start()
            p_copy(to, pc_s, pc_r, kf, c_nb).start()

    refine(y, c, x)
    for k in range(CHUNKS):
        at = place(y, c, 1 - x, k)
        p_copy(at, px_s, px_r, k, x_nb).wait_recv()
        if k % 2 == 0:
            p_copy(at, py_s, py_r, CHUNKS + k // 2, y_nb).start()
        p_copy(at, pc_s, pc_r, CHUNKS + k, c_nb).start()
        at = place(1 - y, c, x, k)
        p_copy(at, py_s, py_r, k, y_nb).wait_recv()
        if k % 2 == 1:
            p_copy(at, px_s, px_r, CHUNKS + k // 2, x_nb).start()
        p_copy(at, pc_s, pc_r, 2 * CHUNKS + k, c_nb).start()
    refine(y, c, 1 - x)
    refine(1 - y, c, x)
    turned = rfull[rows(s * block, block)].T
    rth[...], rtl[...] = split(turned)
    for k in range(CHUNKS):
        at = place(1 - y, c, 1 - x, k)
        if k % 2 == 0:
            p_copy(at, py_s, py_r, CHUNKS + k // 2, y_nb).wait_recv()
        else:
            p_copy(at, px_s, px_r, CHUNKS + k // 2, x_nb).wait_recv()
        p_copy(at, pc_s, pc_r, 3 * CHUNKS + k, c_nb).start()
    refine(1 - y, c, 1 - x)
    others = ((y, x), (y, 1 - x), (1 - y, x), (1 - y, 1 - x))
    for i, (yy, xx) in enumerate(others):
        for k in range(CHUNKS):
            p_copy(place(yy, 1 - c, xx, k), pc_s, pc_r, i * CHUNKS + k, c_nb).wait_recv()
        refine(yy, 1 - c, xx)

    tile = 256 if wide % 256 == 0 else wide
    for n in range(wide // tile):
        at = pl.ds(n * tile, tile)
        done = dot3(oh[...], ol[...], rh[:, at], rl[:, at])
        rdh[:, at], rdl[:, at] = split(done)

    def partial(yy, cc, g):
        at = rows((yy * 2 + cc) * new_rows, new_rows, 16)
        on = pl.ds(g * block, block)
        return dot3(rth[at], rtl[at], rdh[on], rdl[on])

    def c_copy(i, g):
        return copy(sib_out.at[i, g], sib_in.at[i, g], c_s.at[i * local + g], c_r.at[i * local + g], c_nb)

    sides = (1 - y, y)
    for i in range(2):
        for g in range(local):
            sib_out[i, g] = partial(sides[i], 1 - c, g)
            c_copy(i, g).start()
    for g in range(local):
        own[0, g] = partial(sides[0], c, g)

    steps = sorted(range(n_pair), key=lambda m: (-min(m, n_pair - m), m))

    def y_copy(m):
        return copy(y_out.at[m], y_in.at[m], y_s.at[m], y_r.at[m], y_nb)

    for g in range(local):
        c_copy(0, g).wait_recv()
    for m in steps:
        at = rows(lax.rem(p + m, n_pair) * piece, piece)
        y_out[m] = own[0, :, at] + sib_in[0, :, at]
        y_copy(m).start()
    for g in range(local):
        own[1, g] = partial(sides[1], c, g)
        c_copy(1, g).wait_recv()

    def a_copy(m, slot):
        return copy(a_out.at[m], a_in.at[slot], a_s.at[m], a_r.at[m], dev(lax.rem(p + m, n_pair), s))

    for m in steps:
        at = rows(lax.rem(p + m, n_pair) * piece, piece)
        y_copy(m).wait_recv()
        total = own[1, :, at] + sib_in[1, :, at] + y_in[m]
        if m == 0:
            a_in[p] = total
        else:
            a_out[m] = total
            a_copy(m, p).start()
    for m in range(1, n_pair):
        a_copy(m, lax.rem(p - m + n_pair, n_pair)).wait_recv()

    def b_copy(m, slot):
        return copy(b_out.at[m], out_ref.at[:, rows(slot * piece, piece)], b_s.at[m], b_r.at[m],
                    dev(lax.rem(p + m, n_pair), s))

    for m in steps:
        q = lax.rem(p + m, n_pair)
        for j in range(local):
            total = None
            for g in range(n_pair * local):
                term = coup_ref[q * local + j, g] * a_in[g // local, g % local]
                total = term if total is None else total + term
            if m == 0:
                out_ref[j, rows(p * piece, piece)] = total
            else:
                b_out[m, j] = total
        if m:
            b_copy(m, p).start()
    for m in range(1, n_pair):
        b_copy(m, lax.rem(p - m + n_pair, n_pair)).wait_recv()

    for k in range(CHUNKS):
        x_copy(k).wait_send()

        @pl.when(z < depth - 1)
        def _():
            r_copy(k).wait_send()

        @pl.when(z > 0)
        def _():
            l_copy(k).wait_send()

    first = place(y, c, x, 0)
    for i in range(CHUNKS + CHUNKS // 2):
        p_copy(first, px_s, px_r, i, x_nb).wait_send()
        p_copy(first, py_s, py_r, i, y_nb).wait_send()
    for i in range(4 * CHUNKS):
        p_copy(first, pc_s, pc_r, i, c_nb).wait_send()
    for i in range(2):
        for g in range(local):
            c_copy(i, g).wait_send()
    for m in range(n_pair):
        y_copy(m).wait_send()
        if m:
            a_copy(m, p).wait_send()
            b_copy(m, p).wait_send()


def fused(operators, rotation, owner, coupling, n_pair):
    local, block, width = operators.shape
    wide = rotation.shape[1]
    half, new_rows = block // 2, wide // 4
    piece = new_rows // n_pair
    dma = pltpu.SemaphoreType.DMA
    vmem = pltpu.VMEM
    chain = [vmem((half, wide), F32)] * 6
    scratch = [vmem((local * block, width), BF16)] * 2 + chain + [
        vmem((width, wide), F32),
        vmem((width, wide), BF16), vmem((width, wide), BF16),
        vmem((wide, block), BF16), vmem((wide, block), BF16),
        vmem((local * block, wide), BF16), vmem((local * block, wide), BF16),
        vmem((2, local, new_rows, wide), F32),
        vmem((2, local, new_rows, wide), F32),
        vmem((2, local, new_rows, wide), F32),
        vmem((n_pair, local, piece, wide), F32),
        vmem((n_pair, local, piece, wide), F32),
        vmem((n_pair, local, piece, wide), F32),
        vmem((n_pair, local, piece, wide), F32),
        vmem((n_pair, local, piece, wide), F32),
    ]
    links = CHUNKS + CHUNKS // 2
    counts = [CHUNKS] * 6 + [links] * 4 + [4 * CHUNKS] * 2 + [2 * local] * 2 + [n_pair] * 6
    scratch += [dma((count,)) for count in counts]
    smem = pl.BlockSpec(memory_space=pltpu.SMEM)
    in_vmem = pl.BlockSpec(memory_space=pltpu.VMEM)
    return pl.pallas_call(
        functools.partial(kernel, n_pair),
        out_shape=jax.ShapeDtypeStruct((local, new_rows, wide), F32),
        in_specs=[smem, smem, in_vmem, in_vmem],
        out_specs=in_vmem,
        scratch_shapes=scratch,
        compiler_params=pltpu.CompilerParams(
            collective_id=0, has_side_effects=True, vmem_limit_bytes=56 * 1024 * 1024
        ),
    )(owner, coupling, operators, rotation)


def on_device(fits, operators, rotations, sector_owner, slot_pair, sources, integrals, term_count):
    sect_count = lax.axis_size("sect")
    pair_count = lax.axis_size("pair")
    local_ops = operators.shape[0]
    coupling = coupling_matrix(slot_pair, sources, integrals, term_count)
    if fits:
        return fused(operators, rotations[0], sector_owner, coupling, pair_count)
    own_block = broadcast(rotations[0], "pair", sector_owner[0])
    rotation_full = lax.all_gather(own_block, "sect", axis=0, tiled=True)
    width_new = rotation_full.shape[1]
    new_rows = width_new // sect_count
    highest = dict(precision=lax.Precision.HIGHEST, preferred_element_type=jnp.float32)
    right_done = jnp.einsum("oij,jb->oib", operators, rotation_full, **highest)
    columns = lax.dynamic_slice_in_dim(
        rotation_full, lax.axis_index("sect") * new_rows, new_rows, 1
    )
    rotated = jnp.einsum(
        "ia,oib->oab",
        columns,
        lax.all_gather(right_done, "sect", axis=1, tiled=True),
        **highest,
    )
    blocks = rotated.reshape(local_ops, pair_count, -1)
    mixture = jnp.einsum(
        "or,rhn->ohn",
        coupling,
        lax.all_to_all(blocks, "pair", split_axis=1, concat_axis=0, tiled=True),
        **highest,
    )
    result = lax.all_to_all(mixture, "pair", split_axis=0, concat_axis=1, tiled=True)
    return result.reshape(local_ops, new_rows, width_new)


def solution(mesh):
    pair_count, sect_count = mesh.shape["pair"], mesh.shape["sect"]

    def call(operators, rotations, *rest):
        wide = rotations.shape[2]
        fits = sect_count == 4 and pair_count % 2 == 0 and wide % (8 * pair_count * sect_count) == 0
        in_specs = (P("pair", "sect", None), P("pair", "sect", None), P(), P(), P(), P(), P())
        return jax.shard_map(
            functools.partial(on_device, fits), mesh=mesh, in_specs=in_specs,
            out_specs=P("pair", "sect", None), check_vma=False,
        )(operators, rotations, *rest)

    return call
```

```python
import functools

import jax
import jax.numpy as jnp
from jax import lax
from jax.experimental import pallas as pl
from jax.experimental.pallas import tpu as pltpu
from jax.sharding import PartitionSpec as P

F32, BF16 = jnp.float32, jnp.bfloat16
CHUNKS = 4


def broadcast(value, axis, root):
    mine = lax.axis_index(axis) == root
    return lax.psum(jnp.where(mine, value, jnp.zeros_like(value)), axis)


def coupling_matrix(slot_pair, sources, integrals, term_count):
    is_live = lax.broadcasted_iota(jnp.int32, sources.shape, 1) < term_count[:, None]
    weighted = jnp.where(is_live, integrals, jnp.zeros_like(integrals))
    matches = (sources[:, :, None] == slot_pair[None, None, :]).astype(jnp.float32)
    return jnp.sum(weighted[:, :, None] * matches, axis=1)


def split(value):
    high = value.astype(BF16)
    return high, (value - high.astype(F32)).astype(BF16)


def dot3(ah, al, bh, bl):
    dot = functools.partial(jnp.dot, preferred_element_type=F32)
    return dot(ah, bh) + (dot(ah, bl) + dot(al, bh))


def kernel(
    n_pair, owner_ref, slot_ref, count_ref, sources_ref, integrals_ref, ops_in, rot_in, out_ref,
    ops_ref, rot_ref, table, load_sem, oh, ol, xbuf, cand, zr, zl, sr, sl, rfull, rh, rl, rth, rtl, rdh, rdl,
    sib_out, sib_in, own, y_out, y_in, a_out, a_in, b_out,
    x_s, x_r, zr_s, zr_r, zl_s, zl_r, px_s, px_r, py_s, py_r, pc_s, pc_r,
    c_s, c_r, y_s, y_r, a_s, a_r, b_s, b_r,
):
    local, block, width = ops_in.shape
    wide = rot_in.shape[1]
    half = block // 2
    chunk = half // CHUNKS
    new_rows = wide // 4
    piece = new_rows // n_pair
    depth = n_pair // 2
    p, s = lax.axis_index("pair"), lax.axis_index("sect")
    z, x = lax.div(p, 2), lax.rem(p, 2)
    y, c = lax.div(s, 2), lax.rem(s, 2)

    def dev(pp, ss):
        return {"pair": pp, "sect": ss}

    x_nb = dev(p + 1 - 2 * x, s)
    y_nb = dev(p, s + 2 - 4 * y)
    c_nb = dev(p, s + 1 - 2 * c)
    z_up, z_dn = dev(p + 2, s), dev(p - 2, s)

    def copy(src, dst, ssem, rsem, device):
        return pltpu.make_async_remote_copy(
            src_ref=src, dst_ref=dst, send_sem=ssem, recv_sem=rsem,
            device_id=device, device_id_type=pl.DeviceIdType.MESH,
        )

    def rows(start, size, step=8):
        if not isinstance(start, int):
            start = pl.multiple_of(start, step)
        return pl.ds(start, size)

    load_ops = pltpu.make_async_copy(ops_in, ops_ref, load_sem.at[0])
    load_rot = pltpu.make_async_copy(rot_in, rot_ref, load_sem.at[1])
    load_rot.start()
    load_ops.start()
    barrier = pltpu.get_barrier_semaphore()
    for m in range(1, n_pair):
        pl.semaphore_signal(barrier, inc=1, device_id=dev(lax.rem(p + m, n_pair), s),
                            device_id_type=pl.DeviceIdType.MESH)
    for nb in (y_nb, c_nb):
        pl.semaphore_signal(barrier, inc=1, device_id=nb, device_id_type=pl.DeviceIdType.MESH)

    @pl.when(z == 0)
    def _():
        zr[...] = jnp.zeros_like(zr)

    @pl.when(z == depth - 1)
    def _():
        zl[...] = jnp.zeros_like(zl)

    load_rot.wait()
    pl.semaphore_wait(barrier, n_pair + 1)

    def x_copy(k):
        return copy(rot_ref.at[rows((1 - x) * half + k * chunk, chunk)],
                    xbuf.at[rows(k * chunk, chunk)], x_s.at[k], x_r.at[k], x_nb)

    for k in range(CHUNKS):
        x_copy(k).start()

    load_ops.wait()
    for g in range(local):
        for r in range(2):
            at = pl.ds(r * half, half)
            to = pl.ds(g * block + r * half, half)
            oh[to], ol[to] = split(ops_ref[g, at])

    n_ops = sources_ref.shape[0]
    row = lax.broadcasted_iota(jnp.int32, sources_ref.shape, 0)
    entry = lax.broadcasted_iota(jnp.int32, sources_ref.shape, 1)
    live = jnp.zeros(sources_ref.shape, jnp.int32)
    for j in range(n_ops):
        live = jnp.where(row == j, count_ref[j], live)
    weighted = jnp.where(entry < live, integrals_ref[...], 0.0)
    for g in range(n_ops):
        hit = jnp.where(sources_ref[...] == slot_ref[g], weighted, 0.0)
        table[g] = jnp.broadcast_to(jnp.sum(hit, axis=1, keepdims=True), (n_ops, 128))

    owner = owner_ref[0]
    owner_z, owner_x = lax.div(owner, 2), lax.rem(owner, 2)

    def r_copy(k):
        at = rows(k * chunk, chunk)
        return copy(sr.at[at], zr.at[at], zr_s.at[k], zr_r.at[k], z_up)

    def l_copy(k):
        at = rows(k * chunk, chunk)
        return copy(sl.at[at], zl.at[at], zl_s.at[k], zl_r.at[k], z_dn)

    def place(yy, cc, xx, k):
        return rows((yy * 2 + cc) * block + xx * half + k * chunk, chunk)

    def p_copy(at, sends, recvs, i, device):
        return copy(rfull.at[at], rfull.at[at], sends.at[i], recvs.at[i], device)

    def refine(yy, cc, xx):
        at = rows((yy * 2 + cc) * block + xx * half, half, 16)
        rh[at], rl[at] = split(rfull[at])

    far = jnp.maximum(z, depth - 1 - z)
    for t in range(CHUNKS + depth - 1):
        if t < CHUNKS:
            x_copy(t).wait_recv()
            at = rows(t * chunk, chunk)
            mine = rot_ref[rows(x * half + t * chunk, chunk)]
            cand[at] = jnp.where(owner_x == x, mine, xbuf[at])
        kr, kl, kf = t - z, t - (depth - 1 - z), t - far

        @pl.when((kr >= 0) & (kr < CHUNKS))
        def _():
            at = rows(kr * chunk, chunk)

            @pl.when(z > 0)
            def _():
                r_copy(kr).wait_recv()

            @pl.when(z < depth - 1)
            def _():
                sr[at] = jnp.where(owner_z == z, cand[at], zr[at])
                r_copy(kr).start()

        @pl.when((kl >= 0) & (kl < CHUNKS))
        def _():
            at = rows(kl * chunk, chunk)

            @pl.when(z < depth - 1)
            def _():
                l_copy(kl).wait_recv()

            @pl.when(z > 0)
            def _():
                sl[at] = jnp.where(owner_z == z, cand[at], zl[at])
                l_copy(kl).start()

        @pl.when((kf >= 0) & (kf < CHUNKS))
        def _():
            at = rows(kf * chunk, chunk)
            to = place(y, c, x, kf)
            rfull[to] = jnp.where(owner_z == z, cand[at], jnp.where(owner_z < z, zr[at], zl[at]))
            p_copy(to, px_s, px_r, kf, x_nb).start()
            p_copy(to, py_s, py_r, kf, y_nb).start()
            p_copy(to, pc_s, pc_r, kf, c_nb).start()

    refine(y, c, x)
    for k in range(CHUNKS):
        at = place(y, c, 1 - x, k)
        p_copy(at, px_s, px_r, k, x_nb).wait_recv()
        if k % 2 == 0:
            p_copy(at, py_s, py_r, CHUNKS + k // 2, y_nb).start()
        p_copy(at, pc_s, pc_r, CHUNKS + k, c_nb).start()
        at = place(1 - y, c, x, k)
        p_copy(at, py_s, py_r, k, y_nb).wait_recv()
        if k % 2 == 1:
            p_copy(at, px_s, px_r, CHUNKS + k // 2, x_nb).start()
        p_copy(at, pc_s, pc_r, 2 * CHUNKS + k, c_nb).start()
    refine(y, c, 1 - x)
    refine(1 - y, c, x)
    turned = rfull[rows(s * block, block)].T
    rth[...], rtl[...] = split(turned)
    for k in range(CHUNKS):
        at = place(1 - y, c, 1 - x, k)
        if k % 2 == 0:
            p_copy(at, py_s, py_r, CHUNKS + k // 2, y_nb).wait_recv()
        else:
            p_copy(at, px_s, px_r, CHUNKS + k // 2, x_nb).wait_recv()
        p_copy(at, pc_s, pc_r, 3 * CHUNKS + k, c_nb).start()
    refine(1 - y, c, 1 - x)
    others = ((y, x), (y, 1 - x), (1 - y, x), (1 - y, 1 - x))
    for i, (yy, xx) in enumerate(others):
        for k in range(CHUNKS):
            p_copy(place(yy, 1 - c, xx, k), pc_s, pc_r, i * CHUNKS + k, c_nb).wait_recv()
        refine(yy, 1 - c, xx)

    tile = 256 if wide % 256 == 0 else wide
    for n in range(wide // tile):
        at = pl.ds(n * tile, tile)
        done = dot3(oh[...], ol[...], rh[:, at], rl[:, at])
        rdh[:, at], rdl[:, at] = split(done)

    def partial(yy, cc, g):
        at = rows((yy * 2 + cc) * new_rows, new_rows, 16)
        on = pl.ds(g * block, block)
        return dot3(rth[at], rtl[at], rdh[on], rdl[on])

    def c_copy(i, g):
        return copy(sib_out.at[i, g], sib_in.at[i, g], c_s.at[i * local + g], c_r.at[i * local + g], c_nb)

    sides = (1 - y, y)
    for i in range(2):
        for g in range(local):
            sib_out[i, g] = partial(sides[i], 1 - c, g)
            c_copy(i, g).start()
    for g in range(local):
        own[0, g] = partial(sides[0], c, g)

    steps = sorted(range(n_pair), key=lambda m: (-min(m, n_pair - m), m))

    def y_copy(m):
        return copy(y_out.at[m], y_in.at[m], y_s.at[m], y_r.at[m], y_nb)

    for g in range(local):
        c_copy(0, g).wait_recv()
    for m in steps:
        at = rows(lax.rem(p + m, n_pair) * piece, piece)
        y_out[m] = own[0, :, at] + sib_in[0, :, at]
        y_copy(m).start()
    for g in range(local):
        own[1, g] = partial(sides[1], c, g)
        c_copy(1, g).wait_recv()

    def a_copy(m, slot):
        return copy(a_out.at[m], a_in.at[slot], a_s.at[m], a_r.at[m], dev(lax.rem(p + m, n_pair), s))

    for m in steps:
        at = rows(lax.rem(p + m, n_pair) * piece, piece)
        y_copy(m).wait_recv()
        total = own[1, :, at] + sib_in[1, :, at] + y_in[m]
        if m == 0:
            a_in[p] = total
        else:
            a_out[m] = total
            a_copy(m, p).start()
    for m in range(1, n_pair):
        a_copy(m, lax.rem(p - m + n_pair, n_pair)).wait_recv()

    def b_copy(m, slot):
        return copy(b_out.at[m], out_ref.at[:, rows(slot * piece, piece)], b_s.at[m], b_r.at[m],
                    dev(lax.rem(p + m, n_pair), s))

    for m in steps:
        q = lax.rem(p + m, n_pair)
        for n in range(wide // 128):
            at = pl.ds(n * 128, 128)
            for j in range(local):
                total = None
                for g in range(n_ops):
                    term = table[g, pl.ds(q * local + j, 1)] * a_in[g // local, g % local, :, at]
                    total = term if total is None else total + term
                if m == 0:
                    out_ref[j, rows(p * piece, piece), at] = total
                else:
                    b_out[m, j, :, at] = total
        if m:
            b_copy(m, p).start()
    for m in range(1, n_pair):
        b_copy(m, lax.rem(p - m + n_pair, n_pair)).wait_recv()

    for k in range(CHUNKS):
        x_copy(k).wait_send()

        @pl.when(z < depth - 1)
        def _():
            r_copy(k).wait_send()

        @pl.when(z > 0)
        def _():
            l_copy(k).wait_send()

    first = place(y, c, x, 0)
    for i in range(CHUNKS + CHUNKS // 2):
        p_copy(first, px_s, px_r, i, x_nb).wait_send()
        p_copy(first, py_s, py_r, i, y_nb).wait_send()
    for i in range(4 * CHUNKS):
        p_copy(first, pc_s, pc_r, i, c_nb).wait_send()
    for i in range(2):
        for g in range(local):
            c_copy(i, g).wait_send()
    for m in range(n_pair):
        y_copy(m).wait_send()
        if m:
            a_copy(m, p).wait_send()
            b_copy(m, p).wait_send()


def fused(operators, rotation, owner, slot_pair, term_count, sources, integrals, n_pair):
    local, block, width = operators.shape
    wide = rotation.shape[1]
    half, new_rows = block // 2, wide // 4
    piece = new_rows // n_pair
    dma = pltpu.SemaphoreType.DMA
    vmem = pltpu.VMEM
    chain = [vmem((half, wide), F32)] * 6
    scratch = [vmem((local, block, width), F32), vmem((block, wide), F32),
               vmem((local * n_pair, local * n_pair, 128), F32), dma((2,))]
    scratch += [vmem((local * block, width), BF16)] * 2 + chain + [
        vmem((width, wide), F32),
        vmem((width, wide), BF16), vmem((width, wide), BF16),
        vmem((wide, block), BF16), vmem((wide, block), BF16),
        vmem((local * block, wide), BF16), vmem((local * block, wide), BF16),
        vmem((2, local, new_rows, wide), F32),
        vmem((2, local, new_rows, wide), F32),
        vmem((2, local, new_rows, wide), F32),
        vmem((n_pair, local, piece, wide), F32),
        vmem((n_pair, local, piece, wide), F32),
        vmem((n_pair, local, piece, wide), F32),
        vmem((n_pair, local, piece, wide), F32),
        vmem((n_pair, local, piece, wide), F32),
    ]
    links = CHUNKS + CHUNKS // 2
    counts = [CHUNKS] * 6 + [links] * 4 + [4 * CHUNKS] * 2 + [2 * local] * 2 + [n_pair] * 6
    scratch += [dma((count,)) for count in counts]
    smem = pl.BlockSpec(memory_space=pltpu.SMEM)
    in_vmem = pl.BlockSpec(memory_space=pltpu.VMEM)
    return pl.pallas_call(
        functools.partial(kernel, n_pair),
        out_shape=pltpu.VMEM((local, new_rows, wide), F32),
        in_specs=[smem] * 3 + [in_vmem] * 2 + [pl.BlockSpec(memory_space=pl.ANY)] * 2,
        out_specs=in_vmem,
        scratch_shapes=scratch,
        compiler_params=pltpu.CompilerParams(
            collective_id=0, has_side_effects=True, vmem_limit_bytes=56 * 1024 * 1024
        ),
    )(owner, slot_pair, term_count, sources, integrals, operators, rotation)


def on_device(fits, operators, rotations, sector_owner, slot_pair, sources, integrals, term_count):
    sect_count = lax.axis_size("sect")
    pair_count = lax.axis_size("pair")
    local_ops = operators.shape[0]
    if fits:
        return fused(operators, rotations[0], sector_owner, slot_pair, term_count,
                     sources, integrals, pair_count)
    coupling = coupling_matrix(slot_pair, sources, integrals, term_count)
    own_block = broadcast(rotations[0], "pair", sector_owner[0])
    rotation_full = lax.all_gather(own_block, "sect", axis=0, tiled=True)
    width_new = rotation_full.shape[1]
    new_rows = width_new // sect_count
    highest = dict(precision=lax.Precision.HIGHEST, preferred_element_type=jnp.float32)
    right_done = jnp.einsum("oij,jb->oib", operators, rotation_full, **highest)
    columns = lax.dynamic_slice_in_dim(
        rotation_full, lax.axis_index("sect") * new_rows, new_rows, 1
    )
    rotated = jnp.einsum(
        "ia,oib->oab",
        columns,
        lax.all_gather(right_done, "sect", axis=1, tiled=True),
        **highest,
    )
    blocks = rotated.reshape(local_ops, pair_count, -1)
    mixture = jnp.einsum(
        "or,rhn->ohn",
        coupling,
        lax.all_to_all(blocks, "pair", split_axis=1, concat_axis=0, tiled=True),
        **highest,
    )
    result = lax.all_to_all(mixture, "pair", split_axis=0, concat_axis=1, tiled=True)
    return result.reshape(local_ops, new_rows, width_new)


def solution(mesh):
    pair_count, sect_count = mesh.shape["pair"], mesh.shape["sect"]

    def call(operators, rotations, *rest):
        wide = rotations.shape[2]
        fits = sect_count == 4 and pair_count % 2 == 0 and wide % (8 * pair_count * sect_count) == 0
        in_specs = (P("pair", "sect", None), P("pair", "sect", None), P(), P(), P(), P(), P())
        return jax.shard_map(
            functools.partial(on_device, fits), mesh=mesh, in_specs=in_specs,
            out_specs=P("pair", "sect", None), check_vma=False,
        )(operators, rotations, *rest)

    return call
```

```python
import functools

import jax
import jax.numpy as jnp
from jax import lax
from jax.experimental import pallas as pl
from jax.experimental.pallas import tpu as pltpu
from jax.sharding import PartitionSpec as P

F32, BF16 = jnp.float32, jnp.bfloat16
CHUNKS = 4
LAG = 2
PARTS = 2


def broadcast(value, axis, root):
    mine = lax.axis_index(axis) == root
    return lax.psum(jnp.where(mine, value, jnp.zeros_like(value)), axis)


def coupling_matrix(slot_pair, sources, integrals, term_count):
    is_live = lax.broadcasted_iota(jnp.int32, sources.shape, 1) < term_count[:, None]
    weighted = jnp.where(is_live, integrals, jnp.zeros_like(integrals))
    matches = (sources[:, :, None] == slot_pair[None, None, :]).astype(jnp.float32)
    return jnp.sum(weighted[:, :, None] * matches, axis=1)


def split(value):
    high = value.astype(BF16)
    return high, (value - high.astype(F32)).astype(BF16)


def dot3(ah, al, bh, bl):
    dot = functools.partial(jnp.dot, preferred_element_type=F32)
    return dot(ah, bh) + (dot(ah, bl) + dot(al, bh))


def kernel(
    n_pair, owner_ref, slot_ref, count_ref, sources_ref, integrals_ref, ops_in, rot_in, out_ref,
    ops_ref, rot_ref, table, load_sem, oh, ol, xbuf, cand, zr, zl, sr, sl, rfull, rh, rl, rth, rtl, rdh, rdl,
    sib_out, sib_in, own, y_out, y_in, a_out, a_in, b_out,
    x_s, x_r, zr_s, zr_r, zl_s, zl_r, px_s, px_r, py_s, py_r, pc_s, pc_r,
    c_s, c_r, y_s, y_r, a_s, a_r, b_s, b_r,
):
    local, block, width = ops_in.shape
    wide = rot_in.shape[1]
    half = block // 2
    chunk = half // CHUNKS
    new_rows = wide // 4
    piece = new_rows // n_pair
    depth = n_pair // 2
    p, s = lax.axis_index("pair"), lax.axis_index("sect")
    z, x = lax.div(p, 2), lax.rem(p, 2)
    y, c = lax.div(s, 2), lax.rem(s, 2)

    def dev(pp, ss):
        return {"pair": pp, "sect": ss}

    x_nb = dev(p + 1 - 2 * x, s)
    y_nb = dev(p, s + 2 - 4 * y)
    c_nb = dev(p, s + 1 - 2 * c)
    z_up, z_dn = dev(p + 2, s), dev(p - 2, s)

    def copy(src, dst, ssem, rsem, device):
        return pltpu.make_async_remote_copy(
            src_ref=src, dst_ref=dst, send_sem=ssem, recv_sem=rsem,
            device_id=device, device_id_type=pl.DeviceIdType.MESH,
        )

    def rows(start, size, step=8):
        if not isinstance(start, int):
            start = pl.multiple_of(start, step)
        return pl.ds(start, size)

    load_ops = pltpu.make_async_copy(ops_in, ops_ref, load_sem.at[0])
    load_rot = pltpu.make_async_copy(rot_in, rot_ref, load_sem.at[1])
    load_rot.start()
    load_ops.start()
    barrier = pltpu.get_barrier_semaphore()
    for m in range(1, n_pair):
        pl.semaphore_signal(barrier, inc=1, device_id=dev(lax.rem(p + m, n_pair), s),
                            device_id_type=pl.DeviceIdType.MESH)
    for nb in (y_nb, c_nb):
        pl.semaphore_signal(barrier, inc=1, device_id=nb, device_id_type=pl.DeviceIdType.MESH)

    @pl.when(z == 0)
    def _():
        zr[...] = jnp.zeros_like(zr)

    @pl.when(z == depth - 1)
    def _():
        zl[...] = jnp.zeros_like(zl)

    load_rot.wait()
    pl.semaphore_wait(barrier, n_pair + 1)

    def x_copy(k):
        return copy(rot_ref.at[rows((1 - x) * half + k * chunk, chunk)],
                    xbuf.at[rows(k * chunk, chunk)], x_s.at[k], x_r.at[k], x_nb)

    for k in range(CHUNKS):
        x_copy(k).start()

    load_ops.wait()
    for g in range(local):
        for r in range(2):
            at = pl.ds(r * half, half)
            to = pl.ds(g * block + r * half, half)
            oh[to], ol[to] = split(ops_ref[g, at])

    owner = owner_ref[0]
    owner_z, owner_x = lax.div(owner, 2), lax.rem(owner, 2)

    def r_copy(k):
        at = rows(k * chunk, chunk)
        return copy(sr.at[at], zr.at[at], zr_s.at[k], zr_r.at[k], z_up)

    def l_copy(k):
        at = rows(k * chunk, chunk)
        return copy(sl.at[at], zl.at[at], zl_s.at[k], zl_r.at[k], z_dn)

    def place(yy, cc, xx, k):
        return rows((yy * 2 + cc) * block + xx * half + k * chunk, chunk)

    def p_copy(at, sends, recvs, i, device):
        return copy(rfull.at[at], rfull.at[at], sends.at[i], recvs.at[i], device)

    def core_copy(i, xx, yy, cc, k):
        at = rows((yy * 2 + cc) * block + xx * half + k * chunk, 2 * chunk)
        index = i * (CHUNKS // 2) + (k // 2 if isinstance(k, int) else lax.div(k, 2))
        return p_copy(at, pc_s, pc_r, index, c_nb)

    def refine(yy, cc, xx):
        at = rows((yy * 2 + cc) * block + xx * half, half, 16)
        rh[at], rl[at] = split(rfull[at])

    far = jnp.maximum(z, depth - 1 - z)
    for t in range(CHUNKS + depth - 1 + LAG):
        if t < CHUNKS:
            x_copy(t).wait_recv()
            at = rows(t * chunk, chunk)
            mine = rot_ref[rows(x * half + t * chunk, chunk)]
            cand[at] = jnp.where(owner_x == x, mine, xbuf[at])
        kr, kl, kf = t - z, t - (depth - 1 - z), t - far

        @pl.when((kr >= 0) & (kr < CHUNKS))
        def _():
            at = rows(kr * chunk, chunk)

            @pl.when(z > 0)
            def _():
                r_copy(kr).wait_recv()

            @pl.when(z < depth - 1)
            def _():
                sr[at] = jnp.where(owner_z == z, cand[at], zr[at])
                r_copy(kr).start()

        @pl.when((kl >= 0) & (kl < CHUNKS))
        def _():
            at = rows(kl * chunk, chunk)

            @pl.when(z < depth - 1)
            def _():
                l_copy(kl).wait_recv()

            @pl.when(z > 0)
            def _():
                sl[at] = jnp.where(owner_z == z, cand[at], zl[at])
                l_copy(kl).start()

        kg = kf - LAG

        @pl.when((kf >= 0) & (kf < CHUNKS))
        def _():
            at = rows(kf * chunk, chunk)
            to = place(y, c, x, kf)
            rfull[to] = jnp.where(owner_z == z, cand[at], jnp.where(owner_z < z, zr[at], zl[at]))
            p_copy(to, px_s, px_r, kf, x_nb).start()
            p_copy(to, py_s, py_r, kf, y_nb).start()

            @pl.when(lax.rem(kf, 2) == 1)
            def _():
                core_copy(0, x, y, c, kf - 1).start()

        @pl.when((kg >= 0) & (kg < CHUNKS))
        def _():
            from_x, from_y = place(y, c, 1 - x, kg), place(1 - y, c, x, kg)
            p_copy(from_x, px_s, px_r, kg, x_nb).wait_recv()
            p_copy(from_y, py_s, py_r, kg, y_nb).wait_recv()
            onward = CHUNKS + lax.div(kg, 2)

            @pl.when(lax.rem(kg, 2) == 0)
            def _():
                p_copy(from_x, py_s, py_r, onward, y_nb).start()

            @pl.when(lax.rem(kg, 2) == 1)
            def _():
                p_copy(from_y, px_s, px_r, onward, x_nb).start()
                core_copy(1, 1 - x, y, c, kg - 1).start()
                core_copy(2, x, 1 - y, c, kg - 1).start()

    refine(y, c, x)
    for k in range(CHUNKS):
        at = place(1 - y, c, 1 - x, k)
        if k % 2 == 0:
            p_copy(at, py_s, py_r, CHUNKS + k // 2, y_nb).wait_recv()
        else:
            p_copy(at, px_s, px_r, CHUNKS + k // 2, x_nb).wait_recv()
            core_copy(3, 1 - x, 1 - y, c, k - 1).start()
    refine(y, c, 1 - x)
    refine(1 - y, c, x)
    refine(1 - y, c, 1 - x)
    turned = rfull[rows(s * block, block)].T
    rth[...], rtl[...] = split(turned)
    others = ((y, x), (y, 1 - x), (1 - y, x), (1 - y, 1 - x))
    for i, (yy, xx) in enumerate(others):
        for k in range(0, CHUNKS, 2):
            core_copy(i, xx, yy, 1 - c, k).wait_recv()
        refine(yy, 1 - c, xx)

    tile = 256 if wide % 256 == 0 else wide
    for n in range(wide // tile):
        at = pl.ds(n * tile, tile)
        done = dot3(oh[...], ol[...], rh[:, at], rl[:, at])
        rdh[:, at], rdl[:, at] = split(done)

    def partial(yy, cc, g):
        at = rows((yy * 2 + cc) * new_rows, new_rows, 16)
        on = pl.ds(g * block, block)
        return dot3(rth[at], rtl[at], rdh[on], rdl[on])

    def c_copy(i, g):
        return copy(sib_out.at[i, g], sib_in.at[i, g], c_s.at[i * local + g], c_r.at[i * local + g], c_nb)

    sides = (1 - y, y)
    for i in range(2):
        for g in range(local):
            sib_out[i, g] = partial(sides[i], 1 - c, g)
            c_copy(i, g).start()
    for g in range(local):
        own[0, g] = partial(sides[0], c, g)

    steps = sorted(range(n_pair), key=lambda m: (-min(m, n_pair - m), m))

    def columns(u):
        return pl.ds(u * (wide // PARTS), wide // PARTS)

    def y_copy(m, u):
        at, i = columns(u), u * n_pair + m
        return copy(y_out.at[m, :, :, at], y_in.at[m, :, :, at], y_s.at[i], y_r.at[i], y_nb)

    turns = [(u, m) for u in range(PARTS) for m in steps]
    turns_away = [(u, m) for u, m in turns if m]

    for g in range(local):
        c_copy(0, g).wait_recv()
    for u, m in turns:
        at, on = rows(lax.rem(p + m, n_pair) * piece, piece), columns(u)
        y_out[m, :, :, on] = own[0, :, at, on] + sib_in[0, :, at, on]
        y_copy(m, u).start()
    for g in range(local):
        own[1, g] = partial(sides[1], c, g)
        c_copy(1, g).wait_recv()

    def a_copy(m, u, slot):
        at, i = columns(u), u * n_pair + m
        return copy(a_out.at[m, :, :, at], a_in.at[slot, :, :, at], a_s.at[i], a_r.at[i],
                    dev(lax.rem(p + m, n_pair), s))

    for u, m in turns:
        at, on = rows(lax.rem(p + m, n_pair) * piece, piece), columns(u)
        y_copy(m, u).wait_recv()
        total = own[1, :, at, on] + sib_in[1, :, at, on] + y_in[m, :, :, on]
        if m == 0:
            a_in[p, :, :, on] = total
        else:
            a_out[m, :, :, on] = total
            a_copy(m, u, p).start()

    for k in range(CHUNKS):
        x_copy(k).wait_send()

        @pl.when(z < depth - 1)
        def _():
            r_copy(k).wait_send()

        @pl.when(z > 0)
        def _():
            l_copy(k).wait_send()

    first = place(y, c, x, 0)
    for i in range(CHUNKS + CHUNKS // 2):
        p_copy(first, px_s, px_r, i, x_nb).wait_send()
        p_copy(first, py_s, py_r, i, y_nb).wait_send()
    for i in range(4):
        for k in range(0, CHUNKS, 2):
            core_copy(i, x, y, c, k).wait_send()
    for i in range(2):
        for g in range(local):
            c_copy(i, g).wait_send()
    for u, m in turns:
        y_copy(m, u).wait_send()

    n_ops = sources_ref.shape[0]
    row = lax.broadcasted_iota(jnp.int32, sources_ref.shape, 0)
    entry = lax.broadcasted_iota(jnp.int32, sources_ref.shape, 1)
    live = jnp.zeros(sources_ref.shape, jnp.int32)
    for j in range(n_ops):
        live = jnp.where(row == j, count_ref[j], live)
    weighted = jnp.where(entry < live, integrals_ref[...], 0.0)
    for g in range(n_ops):
        hit = jnp.where(sources_ref[...] == slot_ref[g], weighted, 0.0)
        table[g] = jnp.broadcast_to(jnp.sum(hit, axis=1, keepdims=True), (n_ops, 128))

    def b_copy(m, u, slot):
        at, i = columns(u), u * n_pair + m
        return copy(b_out.at[m, :, :, at], out_ref.at[:, rows(slot * piece, piece), at],
                    b_s.at[i], b_r.at[i], dev(lax.rem(p + m, n_pair), s))

    for u in range(PARTS):
        for m in steps:
            if m:
                a_copy(m, u, lax.rem(p - m + n_pair, n_pair)).wait_recv()
        for m in steps:
            q = lax.rem(p + m, n_pair)
            for n in range(wide // PARTS // 128):
                at = pl.ds(u * (wide // PARTS) + n * 128, 128)
                for j in range(local):
                    total = None
                    for g in range(n_ops):
                        term = table[g, pl.ds(q * local + j, 1)] * a_in[g // local, g % local, :, at]
                        total = term if total is None else total + term
                    if m == 0:
                        out_ref[j, rows(p * piece, piece), at] = total
                    else:
                        b_out[m, j, :, at] = total
            if m:
                b_copy(m, u, p).start()
    for u, m in turns_away:
        a_copy(m, u, p).wait_send()
    for u, m in turns_away:
        b_copy(m, u, lax.rem(p - m + n_pair, n_pair)).wait_recv()
    for u, m in turns_away:
        b_copy(m, u, p).wait_send()


def fused(operators, rotation, owner, slot_pair, term_count, sources, integrals, n_pair):
    local, block, width = operators.shape
    wide = rotation.shape[1]
    half, new_rows = block // 2, wide // 4
    piece = new_rows // n_pair
    dma = pltpu.SemaphoreType.DMA
    vmem = pltpu.VMEM
    chain = [vmem((half, wide), F32)] * 6
    scratch = [vmem((local, block, width), F32), vmem((block, wide), F32),
               vmem((local * n_pair, local * n_pair, 128), F32), dma((2,))]
    scratch += [vmem((local * block, width), BF16)] * 2 + chain + [
        vmem((width, wide), F32),
        vmem((width, wide), BF16), vmem((width, wide), BF16),
        vmem((wide, block), BF16), vmem((wide, block), BF16),
        vmem((local * block, wide), BF16), vmem((local * block, wide), BF16),
        vmem((2, local, new_rows, wide), F32),
        vmem((2, local, new_rows, wide), F32),
        vmem((2, local, new_rows, wide), F32),
        vmem((n_pair, local, piece, wide), F32),
        vmem((n_pair, local, piece, wide), F32),
        vmem((n_pair, local, piece, wide), F32),
        vmem((n_pair, local, piece, wide), F32),
        vmem((n_pair, local, piece, wide), F32),
    ]
    links = CHUNKS + CHUNKS // 2
    counts = [CHUNKS] * 6 + [links] * 4 + [2 * CHUNKS] * 2 + [2 * local] * 2 + [PARTS * n_pair] * 6
    scratch += [dma((count,)) for count in counts]
    smem = pl.BlockSpec(memory_space=pltpu.SMEM)
    in_vmem = pl.BlockSpec(memory_space=pltpu.VMEM)
    return pl.pallas_call(
        functools.partial(kernel, n_pair),
        out_shape=pltpu.VMEM((local, new_rows, wide), F32),
        in_specs=[smem] * 3 + [in_vmem] * 2 + [pl.BlockSpec(memory_space=pl.ANY)] * 2,
        out_specs=in_vmem,
        scratch_shapes=scratch,
        compiler_params=pltpu.CompilerParams(
            collective_id=0, has_side_effects=True, vmem_limit_bytes=56 * 1024 * 1024
        ),
    )(owner, slot_pair, term_count, sources, integrals, operators, rotation)


def on_device(fits, operators, rotations, sector_owner, slot_pair, sources, integrals, term_count):
    sect_count = lax.axis_size("sect")
    pair_count = lax.axis_size("pair")
    local_ops = operators.shape[0]
    if fits:
        return fused(operators, rotations[0], sector_owner, slot_pair, term_count,
                     sources, integrals, pair_count)
    coupling = coupling_matrix(slot_pair, sources, integrals, term_count)
    own_block = broadcast(rotations[0], "pair", sector_owner[0])
    rotation_full = lax.all_gather(own_block, "sect", axis=0, tiled=True)
    width_new = rotation_full.shape[1]
    new_rows = width_new // sect_count
    highest = dict(precision=lax.Precision.HIGHEST, preferred_element_type=jnp.float32)
    right_done = jnp.einsum("oij,jb->oib", operators, rotation_full, **highest)
    columns = lax.dynamic_slice_in_dim(
        rotation_full, lax.axis_index("sect") * new_rows, new_rows, 1
    )
    rotated = jnp.einsum(
        "ia,oib->oab",
        columns,
        lax.all_gather(right_done, "sect", axis=1, tiled=True),
        **highest,
    )
    blocks = rotated.reshape(local_ops, pair_count, -1)
    mixture = jnp.einsum(
        "or,rhn->ohn",
        coupling,
        lax.all_to_all(blocks, "pair", split_axis=1, concat_axis=0, tiled=True),
        **highest,
    )
    result = lax.all_to_all(mixture, "pair", split_axis=0, concat_axis=1, tiled=True)
    return result.reshape(local_ops, new_rows, width_new)


def solution(mesh):
    pair_count, sect_count = mesh.shape["pair"], mesh.shape["sect"]

    def call(operators, rotations, *rest):
        wide = rotations.shape[2]
        fits = sect_count == 4 and pair_count % 2 == 0 and wide % (8 * pair_count * sect_count) == 0 and wide % (128 * PARTS) == 0
        in_specs = (P("pair", "sect", None), P("pair", "sect", None), P(), P(), P(), P(), P())
        return jax.shard_map(
            functools.partial(on_device, fits), mesh=mesh, in_specs=in_specs,
            out_specs=P("pair", "sect", None), check_vma=False,
        )(operators, rotations, *rest)

    return call
```
